256 devices in a mesh: dp: 16 (over z, core), expert: 16 (over x, y).
Axes of the slice: x: 4, y: 4, z: 8, core: 2. Of those that a mesh axis runs over, the one named last changes fastest.
Arguments:
- tokens: bfloat16 [32768, 2048], P(('dp', 'expert')), may hold values from -6 to 6
- expert_ids: int32 [32768, 8], P(('dp', 'expert')), may hold values from 0 to 127, as said below
- gate_probs: float32 [32768, 8], P(('dp', 'expert')), may hold values from 0.1 to 1
- cotangent: bfloat16 [32768, 2048], P(('dp', 'expert')), may hold values from -1.5 to 1.5
- expert_weights: bfloat16 [2048, 16, 3, 768], P(None, 'expert'), may hold values from -0.21875 to 0.21875
Outputs:
- mixed: bfloat16 [32768, 2048], P(('dp', 'expert'))
- grad_tokens: bfloat16 [32768, 2048], P(('dp', 'expert'))
- grad_gates: float32 [32768, 8], P(('dp', 'expert'))
- grad_weights: bfloat16 [2048, 16, 3, 768], P('dp', 'expert')
The draws below stay inside these ranges and needn't reach their ends.
Inputs may be any that keep to these rules, and one draw needn't show every extreme that they name: `expert_ids`: each row names 8 different experts. In the rows of one device every expert below 16 is named by 1 to 24 rows, and for every index of dp some such expert is named by exactly 24 rows of each device of that index.
All inputs are finite; a program needn't handle non-finite values.
Results may differ from the reference program's by a relative error of at most 0.0058.
Values may be sent and summed in bfloat16 or wider, within the bound.
A program may use at most 128 MiB of HBM per device.

```python
import math
import jax
import jax.numpy as jnp
from jax import lax

D = 2048
FF = 768
EXPERTS = 128
TOPK = 8
TOK_DEV = 128
HELD = 16
CAP = 24
TOKENS = 32768
N_DP = 16


def draw_expert_ids(key, part):
    blocks = TOKENS // TOK_DEV
    groups = blocks // HELD
    key_hottest, key_counts, key_filler, key_order, key_rolls = jax.random.split(key, 5)
    hottest = jax.random.randint(key_hottest, (groups,), 0, HELD)
    counts = jax.random.randint(key_counts, (groups, HELD, HELD), 1, CAP // 2 + 1)
    is_hottest = jnp.arange(HELD)[None, None, :] == hottest[:, None, None]
    counts = jnp.where(is_hottest, CAP, counts).reshape(blocks, HELD)
    row_index = jnp.arange(TOK_DEV)[:, None]
    slot_index = jnp.arange(TOPK)[None, :]
    position = slot_index * TOK_DEV + row_index
    bounds = jnp.cumsum(counts, axis=1)
    owner = jnp.sum((position[None, :, :, None] >= bounds[:, None, None, :]).astype(jnp.int32), axis=-1)
    totals = bounds[:, -1]
    offsets = jax.random.randint(key_filler, (blocks, TOK_DEV, 1), 0, EXPERTS - HELD)
    filler = HELD + (slot_index[None, :, :] + offsets) % (EXPERTS - HELD)
    chosen = jnp.where(position[None, :, :] < totals[:, None, None], owner, filler)
    order_keys = jax.random.split(key_order, blocks)
    orders = jax.vmap(lambda subkey: jax.random.permutation(subkey, TOK_DEV))(order_keys)
    chosen = jnp.take_along_axis(chosen, orders[:, :, None], axis=1)
    rolls = jax.random.randint(key_rolls, (blocks, TOK_DEV, 1), 0, TOPK)
    columns = (slot_index[None, :, :] + rolls) % TOPK
    chosen = jnp.take_along_axis(chosen, columns, axis=2)
    return chosen.reshape(TOKENS, TOPK).astype(jnp.int32)


def levels(rng, dims, cuts, least, largest):
    level = 1.0
    for dim, parts in cuts:
        heights = jax.random.uniform(jax.random.fold_in(jax.random.fold_in(rng, 6), dim), (parts,), jnp.float32, least / len(cuts), largest / len(cuts))
        level = level * jnp.repeat(jnp.exp(heights), dims[dim] // parts).reshape((-1,) + (1,) * (len(dims) - 1 - dim))
    return level


def normal_values(key, dims, scale, reach, cuts=(), held_as=jnp.bfloat16):
    gain = levels(key, dims, cuts, -0.22, 0.18) if cuts else 1.0
    result = jax.random.normal(key, dims, jnp.float32) * scale * gain
    return jnp.minimum(jnp.maximum(result, -reach), reach).astype(held_as)


def setup_inputs(seed: int = 0) -> dict:
    key_list = jax.random.split(jax.random.key(seed), 6)
    return {
        "tokens": normal_values(key_list[0], (TOKENS, D), 1.0, 6.0, ((0, 256),)),
        "expert_ids": draw_expert_ids(jax.random.fold_in(key_list[5], 71), 0),
        "gate_probs": jnp.clip(jnp.exp(math.log(1.0) - 2.3025851 * jax.random.uniform(key_list[2], (TOKENS, TOPK), jnp.float32) ** levels(key_list[2], (TOKENS, TOPK), ((0, 256),), -0.2, 0.2)), 0.1, 1.0),
        "cotangent": normal_values(key_list[3], (TOKENS, D), 0.25, 1.5, ((0, 256),)),
        "expert_weights": normal_values(key_list[4], (D, HELD, 3, FF), FF ** -0.5, 0.21875, ((1, 16),)),
    }


def expert_rows(x_rows, dy_rows, weights):
    w_gate = weights[:, 0, :]
    w_up = weights[:, 1, :]
    w_down = weights[:, 2, :]
    contract_last = (((1,), (1,)), ((), ()))
    gate_proj = jnp.dot(x_rows, w_gate, preferred_element_type=jnp.float32)
    up_proj = jnp.dot(x_rows, w_up, preferred_element_type=jnp.float32)
    sigmoid_gate = jax.nn.sigmoid(gate_proj)
    silu_gate = gate_proj * sigmoid_gate
    hidden = (silu_gate * up_proj).astype(jnp.bfloat16)
    expert_out = lax.dot_general(hidden, w_down, contract_last, preferred_element_type=jnp.float32).astype(jnp.bfloat16)
    hidden_grad = jnp.dot(dy_rows, w_down, preferred_element_type=jnp.float32)
    gate_grad = (hidden_grad * up_proj * sigmoid_gate * (1.0 + gate_proj * (1.0 - sigmoid_gate))).astype(jnp.bfloat16)
    up_grad = (hidden_grad * silu_gate).astype(jnp.bfloat16)
    token_part = (lax.dot_general(gate_grad, w_gate, contract_last, preferred_element_type=jnp.float32)
                  + lax.dot_general(up_grad, w_up, contract_last, preferred_element_type=jnp.float32)).astype(jnp.bfloat16)
    return expert_out, token_part, hidden, gate_grad, up_grad


def reference(tokens, expert_ids, gate_probs, cotangent, expert_weights):
    assign_total = TOKENS * TOPK
    most_rows = N_DP * HELD * CAP
    flat_ids = expert_ids.reshape(-1)
    flat_probs = gate_probs.reshape(-1)
    token_of = (jnp.arange(assign_total) // TOPK).astype(jnp.int32)
    assign_index = jnp.arange(assign_total).astype(jnp.int32)
    row_index = jnp.arange(most_rows).astype(jnp.int32)
    contract_first = (((0,), (0,)), ((), ()))

    def per_expert(state_in, expert):
        mixed_sum, token_sum, gate_sum = state_in
        chosen = flat_ids == expert
        rank_in = jnp.cumsum(chosen.astype(jnp.int32)) - 1
        target = jnp.where(chosen, rank_in, most_rows).astype(jnp.int32)
        picked = jnp.zeros((most_rows,), jnp.int32).at[target].set(assign_index, mode="drop")
        is_valid = row_index < jnp.sum(chosen.astype(jnp.int32))
        row_tokens = token_of[picked]
        row_probs = jnp.where(is_valid, flat_probs[picked], jnp.zeros((), jnp.float32))
        x_rows = jnp.where(is_valid[:, None], tokens[row_tokens], jnp.zeros((), jnp.bfloat16))
        dy_rows = (row_probs[:, None] * cotangent[row_tokens].astype(jnp.float32)).astype(jnp.bfloat16)
        weights = lax.dynamic_index_in_dim(expert_weights, expert, 1, keepdims=False)
        expert_out, token_part, hidden, gate_grad, up_grad = expert_rows(x_rows, dy_rows, weights)
        out_float = expert_out.astype(jnp.float32)
        mixed_sum = mixed_sum.at[row_tokens].add(row_probs[:, None] * out_float)
        token_sum = token_sum.at[row_tokens].add(
            jnp.where(is_valid[:, None], token_part.astype(jnp.float32), jnp.zeros((), jnp.float32)))
        inner_prod = jnp.sum(out_float * cotangent[row_tokens].astype(jnp.float32), axis=1)
        gate_sum = gate_sum.at[picked].add(jnp.where(is_valid, inner_prod, jnp.zeros((), jnp.float32)))
        weight_grad = jnp.stack([
            lax.dot_general(x_rows, gate_grad, contract_first, preferred_element_type=jnp.float32),
            lax.dot_general(x_rows, up_grad, contract_first, preferred_element_type=jnp.float32),
            lax.dot_general(dy_rows, hidden, contract_first, preferred_element_type=jnp.float32)], axis=1)
        return (mixed_sum, token_sum, gate_sum), weight_grad

    initial = (jnp.zeros((TOKENS, D), jnp.float32), jnp.zeros((TOKENS, D), jnp.float32),
               jnp.zeros((assign_total,), jnp.float32))
    final_state, stacked = lax.scan(per_expert, initial, jnp.arange(HELD).astype(jnp.int32))
    mixed_sum, token_sum, gate_sum = final_state
    grad_weights = jnp.transpose(stacked, (1, 0, 2, 3)).astype(jnp.bfloat16)
    return (mixed_sum.astype(jnp.bfloat16), token_sum.astype(jnp.bfloat16),
            gate_sum.reshape(TOKENS, TOPK), grad_weights)
```

```python
import jax
import jax.numpy as jnp
from jax import lax
from jax.experimental import pallas as pl
from jax.experimental.pallas import tpu as pltpu
from jax.sharding import PartitionSpec as P

CAP = 24
TOK = 128
D = 2048
HALF = 1024
FF = 768
TOPK = 8
NX, NY, NZ = 4, 4, 8
HELD = NX * NY
BLK = 2 * CAP
PACK = HELD * BLK
ROWS = HELD * CAP
TILE = 256
CHUNK = D // (2 * NZ)
PIECE = CHUNK // 2
ORDER = (0, 1, 2)
BF16 = jnp.bfloat16
F32 = jnp.float32
NT = (((1,), (1,)), ((), ()))


def dot(a, b):
    return jnp.dot(a, b, preferred_element_type=F32)


def dot_nt(a, b):
    return lax.dot_general(a, b, NT, preferred_element_type=F32)


def moe_kernel(
    tok, ids, probs, cot, w_hbm,
    mixed, grad_tok, grad_gate, grad_w,
    w, onehot, prob, onehot_t, prob_hi, prob_lo, gate_acc,
    send_x, send_dy, recv_x, recv_dy, recv_out, recv_part,
    xs, dys, x_mine, x_other, dy_mine, dy_other, acts, silus, rights, grads,
    ring_send, ring_recv,
    w_sem, x_ss, x_rs, dy_ss, dy_rs, out_ss, out_rs, part_ss, part_rs,
    sib_ss, sib_rs, ring_ss, ring_rs,
):
    dp, ex = lax.axis_index("dp"), lax.axis_index("expert")
    z, core = lax.div(dp, 2), lax.rem(dp, 2)
    xx, yy = lax.div(ex, NY), lax.rem(ex, NY)

    def peer(i):
        px = lax.rem(xx + lax.div(i, NY), NX)
        py = lax.rem(yy + lax.rem(i, NY), NY)
        return px * NY + py

    sibling = {"dp": z * 2 + (1 - core), "expert": ex}
    after = {"dp": lax.rem(z + 1, NZ) * 2 + core, "expert": ex}
    before = {"dp": lax.rem(z + NZ - 1, NZ) * 2 + core, "expert": ex}

    w_copies = [pltpu.make_async_copy(w_hbm.at[m], w.at[m], w_sem.at[m]) for m in range(3)]
    for c in w_copies:
        c.start()

    barrier = pltpu.get_barrier_semaphore()

    def greet(i, _):
        pl.semaphore_signal(barrier, inc=1, device_id={"dp": dp, "expert": peer(i)})
        return 0

    lax.fori_loop(1, HELD, greet, 0)
    for other in (sibling, after, before):
        pl.semaphore_signal(barrier, inc=1, device_id=other)

    held_id = lax.broadcasted_iota(jnp.int32, (HELD, TOK), 0)
    has = jnp.zeros((HELD, TOK), F32)
    held_prob = jnp.zeros((HELD, TOK), F32)
    for k in range(TOPK):
        hit = ids[k : k + 1, :] == held_id
        has = jnp.where(hit, 1.0, has)
        held_prob = held_prob + jnp.where(hit, probs[k : k + 1, :], 0.0)
    earlier = lax.broadcasted_iota(jnp.int32, (TOK, TOK), 0) < lax.broadcasted_iota(
        jnp.int32, (TOK, TOK), 1
    )
    place = dot(has.astype(BF16), jnp.where(earlier, 1.0, 0.0).astype(BF16))
    place = jnp.where(has > 0.0, place, -1.0)
    slot = lax.broadcasted_iota(jnp.int32, (CAP, TOK), 0).astype(F32)
    zero = jnp.zeros((CAP, TOK), F32)
    for e in range(HELD):
        hit = place[e : e + 1, :] == slot
        one = jnp.where(hit, 1.0, 0.0)
        chance = jnp.where(hit, held_prob[e : e + 1, :], 0.0)
        low, mid, top = BLK * e, BLK * e + CAP, BLK * (e + 1)
        for ref, value in ((onehot, one), (prob, chance)):
            ref[low:mid, 0:TOK] = value
            ref[low:mid, TOK : 2 * TOK] = zero
            ref[mid:top, 0:TOK] = zero
            ref[mid:top, TOK : 2 * TOK] = value

    def columns(j):
        return pl.ds(pl.multiple_of(j * TILE, TILE), TILE)

    def stacked(ref, j):
        right = pl.ds(pl.multiple_of(HALF + j * TILE, TILE), TILE)
        return jnp.concatenate([ref[:, columns(j)], ref[:, right]], axis=0)

    def exchange(i, src, dst, send_sem, recv_sem):
        there = peer(i)
        return pltpu.make_async_remote_copy(
            src_ref=src.at[pl.ds(pl.multiple_of(there * BLK, BLK), BLK)],
            dst_ref=dst.at[pl.ds(pl.multiple_of(ex * BLK, BLK), BLK)],
            send_sem=send_sem.at[i],
            recv_sem=recv_sem.at[ex],
            device_id={"dp": dp, "expert": there},
        )

    def send_all(src, dst, send_sem, recv_sem):
        def one(i, _):
            exchange(i, src, dst, send_sem, recv_sem).start()
            return 0

        lax.fori_loop(1, HELD, one, 0)
        mine = pl.ds(pl.multiple_of(ex * BLK, BLK), BLK)
        pltpu.make_async_copy(src.at[mine], dst.at[mine], recv_sem.at[ex]).start()

    def wait_sent(src, dst, send_sem, recv_sem):
        def one(i, _):
            exchange(i, src, dst, send_sem, recv_sem).wait_send()
            return 0

        lax.fori_loop(1, HELD, one, 0)

    def wait_block(e, dst, recv_sem):
        rows = pl.ds(pl.multiple_of(e * BLK, BLK), BLK)
        pltpu.make_async_copy(dst.at[rows], dst.at[rows], recv_sem.at[e]).wait()

    def pack_x(j, _):
        send_x[:, columns(j)] = dot(onehot[...].astype(BF16), stacked(tok, j)).astype(BF16)
        return 0

    lax.fori_loop(0, HALF // TILE, pack_x, 0)
    pl.semaphore_wait(barrier, HELD - 1 + 3)
    send_all(send_x, recv_x, x_ss, x_rs)

    row_prob = jnp.sum(prob[...], axis=1, keepdims=True)

    def pack_dy(j, _):
        rows = dot(onehot[...].astype(BF16), stacked(cot, j))
        send_dy[:, columns(j)] = (row_prob * rows).astype(BF16)
        return 0

    lax.fori_loop(0, HALF // TILE, pack_dy, 0)
    send_all(send_dy, recv_dy, dy_ss, dy_rs)

    onehot_t[...] = jnp.transpose(onehot[...]).astype(BF16)
    prob_t = jnp.transpose(prob[...])
    high = prob_t.astype(BF16)
    prob_hi[...] = high
    prob_lo[...] = (prob_t - high.astype(F32)).astype(BF16)

    def unpack(recv, recv_sem, full):
        def one(i, _):
            wait_block(2 * i, recv, recv_sem)
            wait_block(2 * i + 1, recv, recv_sem)
            v = recv[pl.ds(pl.multiple_of(i * 2 * BLK, 2 * BLK), 2 * BLK), :].astype(F32)
            rows = pl.ds(pl.multiple_of(i * BLK, BLK), BLK)
            for h in range(2):
                parts = [v[CAP * (2 * b + h) : CAP * (2 * b + h + 1)] for b in range(2)]
                full[rows, HALF * h : HALF * (h + 1)] = jnp.concatenate(parts, axis=0).astype(BF16)
            return 0

        lax.fori_loop(0, HELD // 2, one, 0)

    def flip(full, mine, other):
        def one(c, _):
            at = pl.ds(pl.multiple_of(c * CHUNK, CHUNK), CHUNK)
            for ref, par in ((mine, core), (other, 1 - core)):
                cols = pl.ds(pl.multiple_of((2 * c + par) * CHUNK, CHUNK), CHUNK)
                ref[at, 0:ROWS] = jnp.transpose(full[:, cols])
            return 0

        lax.fori_loop(0, NZ, one, 0)

    def to_sibling(n, src, dst):
        return pltpu.make_async_remote_copy(
            src_ref=src, dst_ref=dst, send_sem=sib_ss.at[n], recv_sem=sib_rs.at[n], device_id=sibling
        )

    own, theirs = pl.ds(0, ROWS), pl.ds(ROWS, ROWS)
    sib = [to_sibling(m, rights.at[m, own], rights.at[m, theirs]) for m in range(3)]
    sib.append(to_sibling(3, x_other, x_mine.at[:, theirs]))
    sib.append(to_sibling(4, dy_other, dy_mine.at[:, theirs]))

    unpack(recv_x, x_rs, xs)
    w_copies[0].wait()
    w_copies[1].wait()

    def project(j, _):
        g = dot(xs[...], w[0, :, columns(j)])
        u = dot(xs[...], w[1, :, columns(j)])
        s = jax.nn.sigmoid(g)
        silu = g * s
        rights[2, own, columns(j)] = (silu * u).astype(BF16)
        acts[:, columns(j)] = u * s * (1.0 + g * (1.0 - s))
        silus[:, columns(j)] = silu
        return 0

    lax.fori_loop(0, FF // TILE, project, 0)
    sib[2].start()
    w_copies[2].wait()
    wait_sent(send_x, recv_x, x_ss, x_rs)

    def repack(ref, j, left, right):
        parts = []
        for s in range(HELD):
            parts += [left[CAP * s : CAP * (s + 1)], right[CAP * s : CAP * (s + 1)]]
        ref[:, columns(j)] = jnp.concatenate(parts, axis=0).astype(BF16)

    def features(j):
        first = pl.ds(pl.multiple_of(j * TILE, TILE), TILE)
        second = pl.ds(pl.multiple_of(HALF + j * TILE, TILE), TILE)
        return first, second

    def expert_out(j, _):
        hidden = rights[2, own, :]
        left, right = [dot_nt(hidden, w[2, rows, :]) for rows in features(j)]
        repack(send_x, j, left, right)
        return 0

    lax.fori_loop(0, HALF // TILE, expert_out, 0)
    flip(xs, x_mine, x_other)
    sib[3].start()

    unpack(recv_dy, dy_rs, dys)
    send_all(send_x, recv_out, out_ss, out_rs)

    def hidden_grad(j, _):
        hg = dot(dys[...], w[2, :, columns(j)])
        rights[0, own, columns(j)] = (hg * acts[:, columns(j)]).astype(BF16)
        rights[1, own, columns(j)] = (hg * silus[:, columns(j)]).astype(BF16)
        return 0

    lax.fori_loop(0, FF // TILE, hidden_grad, 0)
    sib[0].start()
    sib[1].start()
    flip(dys, dy_mine, dy_other)
    sib[4].start()

    def piece(m, way, chunk):
        return grads[m, pl.ds(pl.multiple_of(chunk * CHUNK + way * PIECE, PIECE), PIECE), :]

    def ring(m, way, step):
        n = (step * 3 + m) * 2 + way
        return pltpu.make_async_remote_copy(
            src_ref=ring_send.at[n],
            dst_ref=ring_recv.at[n],
            send_sem=ring_ss.at[n],
            recv_sem=ring_rs.at[n],
            device_id=(after, before)[way],
        )

    def chunk_at(way, distance):
        return lax.rem(z + (NZ - distance if way == 0 else distance), NZ)

    sib[3].wait()
    sib[2].wait()
    for m in ORDER:
        if m < 2:
            sib[m].wait()
        else:
            sib[4].wait()
        lefts = x_mine if m < 2 else dy_mine

        def weight_grad(j, _, m=m, lefts=lefts):
            grads[m, :, columns(j)] = dot(lefts[...], rights[m, :, columns(j)])
            return 0

        lax.fori_loop(0, FF // TILE, weight_grad, 0)
        for way in range(2):
            ring_send[m * 2 + way] = piece(m, way, chunk_at(way, 1)).astype(BF16)
            ring(m, way, 0).start()

    wait_sent(send_dy, recv_dy, dy_ss, dy_rs)

    def token_part(j, _):
        gate_g, up_g = rights[0, own, :], rights[1, own, :]
        left, right = [
            dot_nt(gate_g, w[0, rows, :]) + dot_nt(up_g, w[1, rows, :]) for rows in features(j)
        ]
        repack(send_dy, j, left, right)
        return 0

    lax.fori_loop(0, HALF // TILE, token_part, 0)
    send_all(send_dy, recv_part, part_ss, part_rs)

    def pass_on(step, _):
        for m in ORDER:
            for way in range(2):
                ring(m, way, step).wait_recv()
                n = (step * 3 + m) * 2 + way
                total = ring_recv[n].astype(F32) + piece(m, way, chunk_at(way, step + 2))
                ring_send[n + 6] = total.astype(BF16)
                ring(m, way, step + 1).start()
        return 0

    lax.fori_loop(0, NZ - 2, pass_on, 0)

    def wait_out(e, _):
        wait_block(e, recv_out, out_rs)
        wait_block(e, recv_part, part_rs)
        return 0

    lax.fori_loop(0, HELD, wait_out, 0)
    gate_acc[...] = jnp.zeros_like(gate_acc)

    def combine(j, _):
        back = recv_out[:, columns(j)]
        first, second = features(j)
        mix = dot(prob_hi[...], back) + dot(prob_lo[...], back)
        mixed[:, first] = mix[0:TOK].astype(BF16)
        mixed[:, second] = mix[TOK : 2 * TOK].astype(BF16)
        tokens_g = dot(onehot_t[...], recv_part[:, columns(j)])
        grad_tok[:, first] = tokens_g[0:TOK].astype(BF16)
        grad_tok[:, second] = tokens_g[TOK : 2 * TOK].astype(BF16)
        product = back.astype(F32) * dot(onehot[...].astype(BF16), stacked(cot, j))
        gate_acc[...] += product[:, 0:TOK] + product[:, TOK : 2 * TOK]
        return 0

    lax.fori_loop(0, HALF // TILE, combine, 0)
    inner = jnp.sum(gate_acc[...], axis=1, keepdims=True) * onehot[...]
    result = jnp.zeros((TOPK, TOK), F32)
    for e in range(HELD):
        both = jnp.sum(inner[BLK * e : BLK * (e + 1)], axis=0, keepdims=True)
        value = both[:, 0:TOK] + both[:, TOK : 2 * TOK]
        result = jnp.where(ids[...] == e, value, result)
    grad_gate[...] = result

    for m in ORDER:
        for way in range(2):
            step = NZ - 2
            ring(m, way, step).wait_recv()
            n = (step * 3 + m) * 2 + way
            total = ring_recv[n].astype(F32) + piece(m, way, z)
            grad_w[m, PIECE * way : PIECE * (way + 1), :] = total.astype(BF16)

    wait_sent(send_x, recv_out, out_ss, out_rs)
    wait_sent(send_dy, recv_part, part_ss, part_rs)

    def wait_ring(step, _):
        for m in ORDER:
            for way in range(2):
                ring(m, way, step).wait_send()
        return 0

    lax.fori_loop(0, NZ - 1, wait_ring, 0)


def per_device(tokens, expert_ids, gate_probs, cotangent, expert_weights):
    weights = jnp.transpose(expert_weights[:, 0], (1, 0, 2))
    vmem = pl.BlockSpec(memory_space=pltpu.VMEM)
    pieces = (NZ - 1) * 6
    dma = pltpu.SemaphoreType.DMA
    mixed, grad_tok, grad_gate, grad_w = pl.pallas_call(
        moe_kernel,
        out_shape=(
            jax.ShapeDtypeStruct((TOK, D), BF16),
            jax.ShapeDtypeStruct((TOK, D), BF16),
            jax.ShapeDtypeStruct((TOPK, TOK), F32),
            jax.ShapeDtypeStruct((3, CHUNK, FF), BF16),
        ),
        in_specs=[vmem] * 4 + [pl.BlockSpec(memory_space=pl.ANY)],
        out_specs=(vmem,) * 4,
        scratch_shapes=[
            pltpu.VMEM((3, D, FF), BF16),
            pltpu.VMEM((PACK, 2 * TOK), F32),
            pltpu.VMEM((PACK, 2 * TOK), F32),
            pltpu.VMEM((2 * TOK, PACK), BF16),
            pltpu.VMEM((2 * TOK, PACK), BF16),
            pltpu.VMEM((2 * TOK, PACK), BF16),
            pltpu.VMEM((PACK, TOK), F32),
        ]
        + [pltpu.VMEM((PACK, HALF), BF16)] * 6
        + [pltpu.VMEM((ROWS, D), BF16)] * 2
        + [pltpu.VMEM((HALF, 2 * ROWS), BF16), pltpu.VMEM((HALF, ROWS), BF16)] * 2
        + [pltpu.VMEM((ROWS, FF), F32)] * 2
        + [pltpu.VMEM((3, 2 * ROWS, FF), BF16), pltpu.VMEM((3, HALF, FF), F32)]
        + [pltpu.VMEM((pieces, PIECE, FF), BF16)] * 2
        + [dma((3,))]
        + [dma((HELD,))] * 8
        + [dma((5,))] * 2
        + [dma((pieces,))] * 2,
        compiler_params=pltpu.CompilerParams(
            collective_id=0, has_side_effects=True, vmem_limit_bytes=60 << 20
        ),
    )(tokens, expert_ids.T, gate_probs.T, cotangent, weights)
    return mixed, grad_tok, grad_gate.T, jnp.transpose(grad_w, (1, 0, 2))[:, None]


def solution(mesh):
    rows = P(("dp", "expert"), None)
    return jax.shard_map(
        per_device,
        mesh=mesh,
        in_specs=(rows, rows, rows, rows, P(None, "expert", None, None)),
        out_specs=(rows, rows, rows, P("dp", "expert", None, None)),
        check_vma=False,
    )
```

```python
import jax
import jax.numpy as jnp
from jax import lax
from jax.experimental import pallas as pl
from jax.experimental.pallas import tpu as pltpu
from jax.sharding import PartitionSpec as P

CAP = 24
TOK = 128
D = 2048
HALF = 1024
FF = 768
TOPK = 8
NX, NY, NZ = 4, 4, 8
HELD = NX * NY
BLK = 2 * CAP
PACK = HELD * BLK
ROWS = HELD * CAP
TILE = 256
TILES = HALF // TILE
CHUNK = D // (2 * NZ)
PIECE = CHUNK // 2
HIDDEN_PIECE = FF // 2
ORDER = (2, 0, 1)
OFFSETS = (
    (0, 0), (0, 1), (1, 0), (0, 3), (3, 0), (0, 2), (2, 0), (1, 1),
    (3, 3), (1, 3), (3, 1), (2, 1), (1, 2), (2, 3), (3, 2), (2, 2),
)
BF16 = jnp.bfloat16
F32 = jnp.float32
NT = (((1,), (1,)), ((), ()))


def dot(a, b):
    return jnp.dot(a, b, preferred_element_type=F32)


def dot_nt(a, b):
    return lax.dot_general(a, b, NT, preferred_element_type=F32)


def moe_kernel(
    tok_hbm, ids_hbm, probs_hbm, cot_hbm, w_hbm,
    mixed, grad_tok, grad_gate, grad_w,
    tok, ids, probs, cot,
    w, place, held_prob, onehot, onehot_b, prob, onehot_t, prob_hi, prob_lo, gate_acc,
    send_x, send_dy, recv_x, recv_dy, recv_out, recv_part,
    xs, dys, x_mine, x_other, hidden, hidden_t, acts, silus, rights, grads, grads_t,
    ring_send, ring_recv, ring_send_t, ring_recv_t,
    in_sem, w_sem, x_ss, x_rs, dy_ss, dy_rs, out_ss, out_rs, part_ss, part_rs,
    sib_ss, sib_rs, ring_ss, ring_rs,
):
    dp, ex = lax.axis_index("dp"), lax.axis_index("expert")
    z, core = lax.div(dp, 2), lax.rem(dp, 2)
    xx, yy = lax.div(ex, NY), lax.rem(ex, NY)

    def peer(n, way=1):
        dx, dy = OFFSETS[n]
        if way < 0:
            dx, dy = (NX - dx) % NX, (NY - dy) % NY
        return lax.rem(xx + dx, NX) * NY + lax.rem(yy + dy, NY)

    sibling = {"dp": z * 2 + (1 - core), "expert": ex}
    after = {"dp": lax.rem(z + 1, NZ) * 2 + core, "expert": ex}
    before = {"dp": lax.rem(z + NZ - 1, NZ) * 2 + core, "expert": ex}

    loads = [
        pltpu.make_async_copy(src, dst, in_sem.at[n])
        for n, (src, dst) in enumerate(
            ((ids_hbm, ids), (probs_hbm, probs), (tok_hbm, tok), (cot_hbm, cot))
        )
    ]
    for c in loads:
        c.start()
    w_copies = [
        pltpu.make_async_copy(w_hbm.at[m, :, par], w.at[m, par], w_sem.at[2 * m + par])
        for m in range(3)
        for par in range(2)
    ]

    barrier = pltpu.get_barrier_semaphore()
    for n in range(1, HELD):
        pl.semaphore_signal(barrier, inc=1, device_id={"dp": dp, "expert": peer(n)})
    for other in (sibling, after, before):
        pl.semaphore_signal(barrier, inc=1, device_id=other)

    loads[0].wait()
    loads[1].wait()

    held_id = lax.broadcasted_iota(jnp.int32, (HELD, TOK), 0)
    has = jnp.zeros((HELD, TOK), F32)
    chances = jnp.zeros((HELD, TOK), F32)
    for k in range(TOPK):
        hit = ids[k : k + 1, :] == held_id
        has = jnp.where(hit, 1.0, has)
        chances = chances + jnp.where(hit, probs[k : k + 1, :], 0.0)
    held_prob[...] = chances
    earlier = lax.broadcasted_iota(jnp.int32, (TOK, TOK), 0) < lax.broadcasted_iota(
        jnp.int32, (TOK, TOK), 1
    )
    count = dot(has.astype(BF16), jnp.where(earlier, 1.0, 0.0).astype(BF16))
    place[...] = jnp.where(has > 0.0, count, -1.0)
    slot = lax.broadcasted_iota(jnp.int32, (CAP, TOK), 0).astype(F32)
    zero = jnp.zeros((CAP, TOK), F32)

    def fill(ref, n, value):
        low, mid, top = BLK * n, BLK * n + CAP, BLK * (n + 1)
        ref[low:mid, 0:TOK] = value
        ref[low:mid, TOK : 2 * TOK] = zero
        ref[mid:top, 0:TOK] = zero
        ref[mid:top, TOK : 2 * TOK] = value

    def hits(n):
        return place[pl.ds(peer(n), 1), :] == slot

    def chunk_columns(j, c, h):
        return pl.ds(pl.multiple_of((4 * j + 2 * c + h) * CHUNK, CHUNK), CHUNK)

    def stacked(ref, j):
        halves = [
            jnp.concatenate([ref[:, chunk_columns(j, c, h)] for c in range(2)], axis=1)
            for h in range(2)
        ]
        return jnp.concatenate(halves, axis=0)

    def columns(j):
        return pl.ds(pl.multiple_of(j * TILE, TILE), TILE)

    def exchange(n, way, src, dst, send_sem, recv_sem):
        rows = pl.ds(BLK * n, BLK)
        return pltpu.make_async_remote_copy(
            src_ref=src.at[rows],
            dst_ref=dst.at[rows],
            send_sem=send_sem.at[n],
            recv_sem=recv_sem.at[n],
            device_id={"dp": dp, "expert": peer(n, way)},
        )

    def send_blocks(blocks, way, src, dst, send_sem, recv_sem):
        for n in blocks:
            if n:
                exchange(n, way, src, dst, send_sem, recv_sem).start()
            else:
                mine = pl.ds(0, BLK)
                pltpu.make_async_copy(src.at[mine], dst.at[mine], recv_sem.at[0]).start()

    def wait_sent(way, src, dst, send_sem, recv_sem):
        for n in range(1, HELD):
            exchange(n, way, src, dst, send_sem, recv_sem).wait_send()

    def wait_block(n, dst, recv_sem):
        rows = pl.ds(pl.multiple_of(n * BLK, BLK), BLK)
        pltpu.make_async_copy(dst.at[rows], dst.at[rows], recv_sem.at[n]).wait()

    x_way = (send_x, recv_x, x_ss, x_rs)
    dy_way = (send_dy, recv_dy, dy_ss, dy_rs)
    out_way = (send_x, recv_out, out_ss, out_rs)
    part_way = (send_dy, recv_part, part_ss, part_rs)
    everyone = range(HELD)

    for group in range(2):
        blocks = range(HELD // 2 * group, HELD // 2 * (group + 1))
        for n in blocks:
            fill(onehot, n, jnp.where(hits(n), 1.0, 0.0))
        rows = pl.ds(PACK // 2 * group, PACK // 2)
        onehot_b[rows, :] = onehot[rows, :].astype(BF16)
        if group == 0:
            loads[2].wait()
            for c in w_copies:
                c.start()

        def pack_x(j, _, rows=rows):
            send_x[rows, columns(j)] = dot(onehot_b[rows, :], stacked(tok, j)).astype(BF16)
            return 0

        lax.fori_loop(0, TILES, pack_x, 0)
        if group == 0:
            pl.semaphore_wait(barrier, HELD - 1 + 3)
        send_blocks(blocks, 1, *x_way)

    for n in everyone:
        fill(prob, n, jnp.where(hits(n), held_prob[pl.ds(peer(n), 1), :], 0.0))
    row_prob = jnp.sum(prob[...], axis=1, keepdims=True)
    loads[3].wait()

    def pack_dy(j, _):
        picked = dot(onehot_b[...], stacked(cot, j))
        send_dy[:, columns(j)] = (row_prob * picked).astype(BF16)
        return 0

    lax.fori_loop(0, TILES, pack_dy, 0)
    send_blocks(everyone, 1, *dy_way)

    onehot_t[...] = jnp.transpose(onehot[...]).astype(BF16)
    prob_t = jnp.transpose(prob[...])
    high = prob_t.astype(BF16)
    prob_hi[...] = high
    prob_lo[...] = (prob_t - high.astype(F32)).astype(BF16)

    own, theirs = pl.ds(0, ROWS), pl.ds(ROWS, ROWS)

    def to_sibling(n, src, dst):
        return pltpu.make_async_remote_copy(
            src_ref=src, dst_ref=dst, send_sem=sib_ss.at[n], recv_sem=sib_rs.at[n], device_id=sibling
        )

    x_over = to_sibling(0, x_other, x_mine.at[:, theirs])
    hidden_over = to_sibling(1, hidden_t.at[:, own], hidden_t.at[:, theirs])

    def dy_over(i):
        rows = pl.ds(pl.multiple_of(i * BLK, BLK), BLK)
        there = pl.ds(pl.multiple_of(ROWS + i * BLK, BLK), BLK)
        return to_sibling(2 + i, dys.at[1 - core, rows], dys.at[1 - core, there])

    def grad_over(m, j):
        src, dst = rights.at[m, own, columns(j)], rights.at[m, theirs, columns(j)]
        return to_sibling(2 + HELD // 2 + 3 * m + j, src, dst)

    def unpack(recv, recv_sem, full, then=None):
        def one(i, _):
            wait_block(2 * i, recv, recv_sem)
            wait_block(2 * i + 1, recv, recv_sem)
            v = recv[pl.ds(pl.multiple_of(i * 2 * BLK, 2 * BLK), 2 * BLK), :].astype(F32)
            rows = pl.ds(pl.multiple_of(i * BLK, BLK), BLK)
            for h in range(2):
                parts = [v[CAP * (2 * b + h) : CAP * (2 * b + h + 1)] for b in range(2)]
                full[h, rows, :] = jnp.concatenate(parts, axis=0).astype(BF16)
            if then is not None:
                then(i).start()
            return 0

        lax.fori_loop(0, HELD // 2, one, 0)

    def weight(m, h, j):
        return w[m, h, :, :, columns(j)].reshape(HALF, TILE)

    unpack(recv_x, x_rs, xs)
    for c in w_copies:
        c.wait()

    def project(j, _):
        g = dot(xs[0], weight(0, 0, j)) + dot(xs[1], weight(0, 1, j))
        u = dot(xs[0], weight(1, 0, j)) + dot(xs[1], weight(1, 1, j))
        s = jax.nn.sigmoid(g)
        silu = g * s
        units = (silu * u).astype(BF16)
        hidden[:, columns(j)] = units
        hidden_t[columns(j), own] = jnp.transpose(units)
        acts[:, columns(j)] = u * s * (1.0 + g * (1.0 - s))
        silus[:, columns(j)] = silu
        return 0

    lax.fori_loop(0, FF // TILE, project, 0)
    hidden_over.start()

    def flip(c, _):
        at = pl.ds(pl.multiple_of(c * CHUNK, CHUNK), CHUNK)
        x_mine[at, own] = jnp.transpose(xs[core, :, at])
        x_other[at, :] = jnp.transpose(xs[1 - core, :, at])
        return 0

    lax.fori_loop(0, NZ, flip, 0)
    x_over.start()
    wait_sent(1, *x_way)

    def repack(ref, j, left, right):
        parts = []
        for n in range(HELD):
            parts += [left[CAP * n : CAP * (n + 1)], right[CAP * n : CAP * (n + 1)]]
        ref[:, columns(j)] = jnp.concatenate(parts, axis=0).astype(BF16)

    def weight_rows(m, h, j):
        return w[m, h, pl.ds(2 * j, 2)].reshape(TILE, FF)

    def expert_out(j, _):
        left, right = [dot_nt(hidden[...], weight_rows(2, h, j)) for h in range(2)]
        repack(send_x, j, left, right)
        return 0

    lax.fori_loop(0, TILES, expert_out, 0)
    unpack(recv_dy, dy_rs, dys, dy_over)
    send_blocks(everyone, -1, *out_way)

    for j in range(FF // TILE):
        hg = dot(dys[0, own, :], weight(2, 0, j)) + dot(dys[1, own, :], weight(2, 1, j))
        rights[0, own, columns(j)] = (hg * acts[:, columns(j)]).astype(BF16)
        rights[1, own, columns(j)] = (hg * silus[:, columns(j)]).astype(BF16)
        grad_over(0, j).start()
        grad_over(1, j).start()

    def piece(m, way, chunk):
        if m == 2:
            cols = pl.ds(pl.multiple_of(chunk * CHUNK, CHUNK), CHUNK)
            return grads_t[HIDDEN_PIECE * way : HIDDEN_PIECE * (way + 1), cols]
        return grads[m, pl.ds(pl.multiple_of(chunk * CHUNK + way * PIECE, PIECE), PIECE), :]

    def slots(m, way, step):
        if m == 2:
            return ring_send_t, ring_recv_t, step * 2 + way
        return ring_send, ring_recv, (step * 2 + m) * 2 + way

    def ring(m, way, step):
        src, dst, n = slots(m, way, step)
        k = (step * 3 + m) * 2 + way
        return pltpu.make_async_remote_copy(
            src_ref=src.at[n],
            dst_ref=dst.at[n],
            send_sem=ring_ss.at[k],
            recv_sem=ring_rs.at[k],
            device_id=(after, before)[way],
        )

    def chunk_at(way, distance):
        return lax.rem(z + (NZ - distance if way == 0 else distance), NZ)

    def begin(m):
        for way in range(2):
            src, _, n = slots(m, way, 0)
            src[n] = piece(m, way, chunk_at(way, 1)).astype(BF16)
            ring(m, way, 0).start()

    hidden_over.wait()
    for i in range(HELD // 2):
        dy_over(i).wait()

    def down_grad(j, _):
        grads_t[:, columns(j)] = dot(hidden_t[...], dys[core, :, columns(j)])
        return 0

    lax.fori_loop(0, TILES, down_grad, 0)
    begin(2)
    x_over.wait()
    for m in range(2):
        for j in range(FF // TILE):
            grad_over(m, j).wait()

        def weight_grad(j, _, m=m):
            grads[m, :, columns(j)] = dot(x_mine[...], rights[m, :, columns(j)])
            return 0

        lax.fori_loop(0, FF // TILE, weight_grad, 0)
        begin(m)

    wait_sent(1, *dy_way)

    def token_part(j, _):
        gate_g, up_g = rights[0, own, :], rights[1, own, :]
        left, right = [
            dot_nt(gate_g, weight_rows(0, h, j)) + dot_nt(up_g, weight_rows(1, h, j))
            for h in range(2)
        ]
        repack(send_dy, j, left, right)
        return 0

    lax.fori_loop(0, TILES, token_part, 0)
    send_blocks(everyone, -1, *part_way)

    def pass_on(step, _):
        for m in ORDER:
            for way in range(2):
                ring(m, way, step).wait_recv()
                src, dst, n = slots(m, way, step)
                total = dst[n].astype(F32) + piece(m, way, chunk_at(way, step + 2))
                src[n + (2 if m == 2 else 4)] = total.astype(BF16)
                ring(m, way, step + 1).start()
        return 0

    lax.fori_loop(0, NZ - 2, pass_on, 0)

    for n in everyone:
        wait_block(n, recv_out, out_rs)
        wait_block(n, recv_part, part_rs)
    gate_acc[...] = jnp.zeros_like(gate_acc)

    def spread(ref, j, value):
        for h in range(2):
            for c in range(2):
                ref[:, chunk_columns(j, c, h)] = value[
                    TOK * h : TOK * (h + 1), CHUNK * c : CHUNK * (c + 1)
                ].astype(BF16)

    def combine(j, _):
        back = recv_out[:, columns(j)]
        spread(mixed, j, dot(prob_hi[...], back) + dot(prob_lo[...], back))
        spread(grad_tok, j, dot(onehot_t[...], recv_part[:, columns(j)]))
        product = back.astype(F32) * dot(onehot_b[...], stacked(cot, j))
        gate_acc[...] += product[:, 0:TOK] + product[:, TOK : 2 * TOK]
        return 0

    lax.fori_loop(0, TILES, combine, 0)
    inner = jnp.sum(gate_acc[...], axis=1, keepdims=True) * onehot[...]
    result = jnp.zeros((TOPK, TOK), F32)
    for n in everyone:
        both = jnp.sum(inner[BLK * n : BLK * (n + 1)], axis=0, keepdims=True)
        value = both[:, 0:TOK] + both[:, TOK : 2 * TOK]
        result = jnp.where(ids[...] == peer(n), value, result)
    grad_gate[...] = result

    for m in ORDER:
        for way in range(2):
            ring(m, way, NZ - 2).wait_recv()
            _, dst, n = slots(m, way, NZ - 2)
            total = dst[n].astype(F32) + piece(m, way, z)
            if m == 2:
                cols = pl.ds(HIDDEN_PIECE * way, HIDDEN_PIECE)
                grad_w[m, :, cols] = jnp.transpose(total).astype(BF16)
            else:
                grad_w[m, PIECE * way : PIECE * (way + 1), :] = total.astype(BF16)

    wait_sent(-1, *out_way)
    wait_sent(-1, *part_way)

    def wait_ring(step, _):
        for m in ORDER:
            for way in range(2):
                ring(m, way, step).wait_send()
        return 0

    lax.fori_loop(0, NZ - 1, wait_ring, 0)


def hand_out(*refs):
    ins, outs, sem = refs[:4], refs[4:8], refs[8]
    copies = [pltpu.make_async_copy(a, b, sem.at[n]) for n, (a, b) in enumerate(zip(ins, outs))]
    for c in copies:
        c.start()
    for c in copies:
        c.wait()


def per_device(tokens, expert_ids, gate_probs, cotangent, expert_weights):
    weights = jnp.transpose(expert_weights[:, 0], (1, 0, 2)).reshape(3, NZ, 2, CHUNK, FF)
    anywhere = pl.BlockSpec(memory_space=pl.ANY)
    dma = pltpu.SemaphoreType.DMA
    vmem = pltpu.VMEM
    results = (
        jax.ShapeDtypeStruct((TOK, D), BF16),
        jax.ShapeDtypeStruct((TOK, D), BF16),
        jax.ShapeDtypeStruct((TOPK, TOK), F32),
        jax.ShapeDtypeStruct((3, CHUNK, FF), BF16),
    )
    made = pl.pallas_call(
        moe_kernel,
        out_shape=tuple(vmem(r.shape, r.dtype) for r in results),
        in_specs=[anywhere] * 5,
        out_specs=(pl.BlockSpec(memory_space=pltpu.VMEM),) * 4,
        scratch_shapes=[
            vmem((TOK, D), BF16),
            vmem((TOPK, TOK), jnp.int32),
            vmem((TOPK, TOK), F32),
            vmem((TOK, D), BF16),
        ]
        + [
            vmem((3, 2, NZ, CHUNK, FF), BF16),
            vmem((HELD, TOK), F32),
            vmem((HELD, TOK), F32),
            vmem((PACK, 2 * TOK), F32),
            vmem((PACK, 2 * TOK), BF16),
            vmem((PACK, 2 * TOK), F32),
        ]
        + [vmem((2 * TOK, PACK), BF16)] * 3
        + [vmem((PACK, TOK), F32)]
        + [vmem((PACK, HALF), BF16)] * 6
        + [
            vmem((2, ROWS, HALF), BF16),
            vmem((2, 2 * ROWS, HALF), BF16),
            vmem((HALF, 2 * ROWS), BF16),
            vmem((HALF, ROWS), BF16),
            vmem((ROWS, FF), BF16),
            vmem((FF, 2 * ROWS), BF16),
            vmem((ROWS, FF), F32),
            vmem((ROWS, FF), F32),
            vmem((2, 2 * ROWS, FF), BF16),
            vmem((2, HALF, FF), F32),
            vmem((FF, HALF), F32),
        ]
        + [vmem(((NZ - 1) * 4, PIECE, FF), BF16)] * 2
        + [vmem(((NZ - 1) * 2, HIDDEN_PIECE, CHUNK), BF16)] * 2
        + [dma((4,)), dma((6,))]
        + [dma((HELD,))] * 8
        + [dma((2 + HELD // 2 + 6,))] * 2
        + [dma(((NZ - 1) * 6,))] * 2,
        compiler_params=pltpu.CompilerParams(
            collective_id=0, has_side_effects=True, vmem_limit_bytes=60 << 20
        ),
    )(tokens, expert_ids.T, gate_probs.T, cotangent, weights)
    made = [pltpu.with_memory_space_constraint(m, pltpu.VMEM) for m in made]
    mixed, grad_tok, grad_gate, grad_w = pl.pallas_call(
        hand_out,
        out_shape=results,
        in_specs=[pl.BlockSpec(memory_space=pltpu.VMEM)] * 4,
        out_specs=(anywhere,) * 4,
        scratch_shapes=[dma((4,))],
    )(*made)
    return mixed, grad_tok, grad_gate.T, jnp.transpose(grad_w, (1, 0, 2))[:, None]


def solution(mesh):
    rows = P(("dp", "expert"), None)
    return jax.shard_map(
        per_device,
        mesh=mesh,
        in_specs=(rows, rows, rows, rows, P(None, "expert", None, None)),
        out_specs=(rows, rows, rows, P("dp", "expert", None, None)),
        check_vma=False,
    )
```

```python
import jax
import jax.numpy as jnp
from jax import lax
from jax.experimental import pallas as pl
from jax.experimental.pallas import tpu as pltpu
from jax.sharding import PartitionSpec as P

CAP = 24
TOK = 128
D = 2048
HALF = 1024
FF = 768
TOPK = 8
NX, NY, NZ = 4, 4, 8
HELD = NX * NY
BLK = 2 * CAP
PACK = HELD * BLK
ROWS = HELD * CAP
TILE = 256
TILES = HALF // TILE
CHUNK = D // (2 * NZ)
PIECE = CHUNK // 2
HIDDEN_PIECE = FF // 2
PART = HALF // 2
OFFSETS = (
    (0, 0), (2, 2), (0, 2), (2, 0), (1, 2), (2, 1), (3, 2), (2, 3),
    (1, 1), (3, 3), (1, 3), (3, 1), (0, 1), (1, 0), (0, 3), (3, 0),
)
BF16 = jnp.bfloat16
F32 = jnp.float32
NT = (((1,), (1,)), ((), ()))


def dot(a, b):
    return jnp.dot(a, b, preferred_element_type=F32)


def dot_nt(a, b):
    return lax.dot_general(a, b, NT, preferred_element_type=F32)


def moe_kernel(
    tok_hbm, ids_hbm, probs_hbm, cot_hbm, w_hbm,
    mixed, grad_tok, grad_gate, grad_w,
    tok, ids, probs, cot,
    w, place, held_prob, onehot, onehot_b, prob, onehot_t, prob_hi, prob_lo, gate_acc,
    send_x, send_dy, send_part, recv_x, recv_dy, recv_out, recv_part,
    xs, dys, x_mine, x_other, hidden, hidden_t, acts, silus, partial, rights, grads, grads_t,
    ring_send, ring_recv, ring_send_t, ring_recv_t,
    in_sem, w_sem, x_ss, x_rs, dy_ss, dy_rs, late_ss, late_rs, out_ss, out_rs, part_ss, part_rs,
    sib_ss, sib_rs, ring_ss, ring_rs,
):
    dp, ex = lax.axis_index("dp"), lax.axis_index("expert")
    z, core = lax.div(dp, 2), lax.rem(dp, 2)
    xx, yy = lax.div(ex, NY), lax.rem(ex, NY)

    def peer(n, way=1):
        dx, dy = OFFSETS[n]
        if way < 0:
            dx, dy = (NX - dx) % NX, (NY - dy) % NY
        return lax.rem(xx + dx, NX) * NY + lax.rem(yy + dy, NY)

    sibling = {"dp": z * 2 + (1 - core), "expert": ex}
    after = {"dp": lax.rem(z + 1, NZ) * 2 + core, "expert": ex}
    before = {"dp": lax.rem(z + NZ - 1, NZ) * 2 + core, "expert": ex}

    loads = [
        pltpu.make_async_copy(src, dst, in_sem.at[n])
        for n, (src, dst) in enumerate(
            ((ids_hbm, ids), (probs_hbm, probs), (tok_hbm, tok), (cot_hbm, cot))
        )
    ]
    for c in loads:
        c.start()
    def near_chunk(j, c):
        if c == 0:
            return lax.rem(z + NZ - 1 - j, NZ)
        return lax.rem(z + 1 + j + NZ // 2 * (j // (TILES - 1)), NZ)

    w_copies = [
        pltpu.make_async_copy(w_hbm.at[m, :, h], w.at[m, h], w_sem.at[2 * m + h])
        for m in range(2)
        for h in range(2)
    ]
    w_copies += [
        pltpu.make_async_copy(
            w_hbm.at[2, near_chunk(j, c), h], w.at[2, h, 2 * j + c], w_sem.at[4 + (2 * j + c) * 2 + h]
        )
        for j in range(TILES)
        for c in range(2)
        for h in range(2)
    ]

    barrier = pltpu.get_barrier_semaphore()
    for n in range(1, HELD):
        pl.semaphore_signal(barrier, inc=1, device_id={"dp": dp, "expert": peer(n)})
    for other in (sibling, after, before):
        pl.semaphore_signal(barrier, inc=1, device_id=other)

    loads[0].wait()
    loads[1].wait()

    held_id = lax.broadcasted_iota(jnp.int32, (HELD, TOK), 0)
    has = jnp.zeros((HELD, TOK), F32)
    chances = jnp.zeros((HELD, TOK), F32)
    for k in range(TOPK):
        hit = ids[k : k + 1, :] == held_id
        has = jnp.where(hit, 1.0, has)
        chances = chances + jnp.where(hit, probs[k : k + 1, :], 0.0)
    held_prob[...] = chances
    earlier = lax.broadcasted_iota(jnp.int32, (TOK, TOK), 0) < lax.broadcasted_iota(
        jnp.int32, (TOK, TOK), 1
    )
    count = dot(has.astype(BF16), jnp.where(earlier, 1.0, 0.0).astype(BF16))
    place[...] = jnp.where(has > 0.0, count, -1.0)
    slot = lax.broadcasted_iota(jnp.int32, (CAP, TOK), 0).astype(F32)
    zero = jnp.zeros((CAP, TOK), F32)

    def fill(ref, n, value):
        low, mid, top = BLK * n, BLK * n + CAP, BLK * (n + 1)
        ref[low:mid, 0:TOK] = value
        ref[low:mid, TOK : 2 * TOK] = zero
        ref[mid:top, 0:TOK] = zero
        ref[mid:top, TOK : 2 * TOK] = value

    def hits(n):
        return place[pl.ds(peer(n), 1), :] == slot

    def chunk_columns(j, c, h):
        return pl.ds(pl.multiple_of((4 * j + 2 * c + h) * CHUNK, CHUNK), CHUNK)

    def near_columns(j, c, h):
        return pl.ds(pl.multiple_of((2 * near_chunk(j, c) + h) * CHUNK, CHUNK), CHUNK)

    def stacked(ref, j, at):
        halves = [
            jnp.concatenate([ref[:, at(j, c, h)] for c in range(2)], axis=1) for h in range(2)
        ]
        return jnp.concatenate(halves, axis=0)

    def columns(j):
        return pl.ds(pl.multiple_of(j * TILE, TILE), TILE)

    def exchange(n, way, src, dst, send_sem, recv_sem):
        rows = pl.ds(BLK * n, BLK)
        return pltpu.make_async_remote_copy(
            src_ref=src.at[rows],
            dst_ref=dst.at[rows],
            send_sem=send_sem.at[n],
            recv_sem=recv_sem.at[n],
            device_id={"dp": dp, "expert": peer(n, way)},
        )

    def send_blocks(blocks, way, src, dst, send_sem, recv_sem):
        for n in blocks:
            if n:
                exchange(n, way, src, dst, send_sem, recv_sem).start()
            else:
                mine = pl.ds(0, BLK)
                pltpu.make_async_copy(src.at[mine], dst.at[mine], recv_sem.at[0]).start()

    def wait_sent(way, src, dst, send_sem, recv_sem):
        for n in range(1, HELD):
            exchange(n, way, src, dst, send_sem, recv_sem).wait_send()

    def wait_block(n, dst, recv_sem):
        rows = pl.ds(pl.multiple_of(n * BLK, BLK), BLK)
        pltpu.make_async_copy(dst.at[rows], dst.at[rows], recv_sem.at[n]).wait()

    x_way = (send_x, recv_x, x_ss, x_rs)
    dy_ways = (
        (send_dy.at[0], recv_dy.at[0], dy_ss, dy_rs),
        (send_dy.at[1], recv_dy.at[1], late_ss, late_rs),
    )
    out_way = (send_x, recv_out, out_ss, out_rs)
    part_way = (send_part, recv_part, part_ss, part_rs)
    everyone = range(HELD)

    for group in range(2):
        blocks = range(HELD // 2 * group, HELD // 2 * (group + 1))
        for n in blocks:
            fill(onehot, n, jnp.where(hits(n), 1.0, 0.0))
        rows = pl.ds(PACK // 2 * group, PACK // 2)
        onehot_b[rows, :] = onehot[rows, :].astype(BF16)
        if group == 0:
            loads[2].wait()
            for c in w_copies:
                c.start()

        def pack_x(j, _, rows=rows):
            send_x[rows, columns(j)] = dot(onehot_b[rows, :], stacked(tok, j, chunk_columns)).astype(BF16)
            return 0

        lax.fori_loop(0, TILES, pack_x, 0)
        if group == 0:
            pl.semaphore_wait(barrier, HELD - 1 + 3)
        send_blocks(blocks, 1, *x_way)

    for n in everyone:
        fill(prob, n, jnp.where(hits(n), held_prob[pl.ds(peer(n), 1), :], 0.0))
    row_prob = jnp.sum(prob[...], axis=1, keepdims=True)
    loads[3].wait()

    for part in range(2):
        for j in range(TILES // 2):
            picked = dot(onehot_b[...], stacked(cot, part * TILES // 2 + j, near_columns))
            send_dy[part, :, columns(j)] = (row_prob * picked).astype(BF16)
        send_blocks(everyone, 1, *dy_ways[part])

    onehot_t[...] = jnp.transpose(onehot[...]).astype(BF16)
    prob_t = jnp.transpose(prob[...])
    high = prob_t.astype(BF16)
    prob_hi[...] = high
    prob_lo[...] = (prob_t - high.astype(F32)).astype(BF16)

    own, theirs = pl.ds(0, ROWS), pl.ds(ROWS, ROWS)

    def to_sibling(n, src, dst):
        return pltpu.make_async_remote_copy(
            src_ref=src, dst_ref=dst, send_sem=sib_ss.at[n], recv_sem=sib_rs.at[n], device_id=sibling
        )

    x_over = to_sibling(0, x_other, x_mine.at[:, theirs])
    hidden_over = to_sibling(1, hidden_t.at[:, own], hidden_t.at[:, theirs])

    def dy_over(part, i):
        rows = pl.ds(pl.multiple_of(i * BLK, BLK), BLK)
        there = pl.ds(pl.multiple_of(ROWS + i * BLK, BLK), BLK)
        cols = pl.ds(PART * part, PART)
        src, dst = dys.at[1 - core, rows, cols], dys.at[1 - core, there, cols]
        return to_sibling(2 + HELD // 2 * part + i, src, dst)

    def grad_over(m, j):
        src, dst = rights.at[m, own, columns(j)], rights.at[m, theirs, columns(j)]
        return to_sibling(2 + HELD + 3 * m + j, src, dst)

    def unpack(recv, recv_sem, full, cols, then=None):
        def one(i, _):
            wait_block(2 * i, recv, recv_sem)
            wait_block(2 * i + 1, recv, recv_sem)
            v = recv[pl.ds(pl.multiple_of(i * 2 * BLK, 2 * BLK), 2 * BLK), :].astype(F32)
            rows = pl.ds(pl.multiple_of(i * BLK, BLK), BLK)
            for h in range(2):
                parts = [v[CAP * (2 * b + h) : CAP * (2 * b + h + 1)] for b in range(2)]
                full[h, rows, cols] = jnp.concatenate(parts, axis=0).astype(BF16)
            if then is not None:
                then(i).start()
            return 0

        lax.fori_loop(0, HELD // 2, one, 0)

    def weight(m, h, j):
        return w[m, h, :, :, columns(j)].reshape(HALF, TILE)

    unpack(recv_x, x_rs, xs, pl.ds(0, HALF))
    for c in w_copies:
        c.wait()

    def project(j, _):
        g = dot(xs[0], weight(0, 0, j)) + dot(xs[1], weight(0, 1, j))
        u = dot(xs[0], weight(1, 0, j)) + dot(xs[1], weight(1, 1, j))
        s = jax.nn.sigmoid(g)
        silu = g * s
        units = (silu * u).astype(BF16)
        hidden[:, columns(j)] = units
        hidden_t[columns(j), own] = jnp.transpose(units)
        acts[:, columns(j)] = u * s * (1.0 + g * (1.0 - s))
        silus[:, columns(j)] = silu
        return 0

    lax.fori_loop(0, FF // TILE, project, 0)
    hidden_over.start()

    def flip(c, _):
        at = pl.ds(pl.multiple_of(c * CHUNK, CHUNK), CHUNK)
        x_mine[at, own] = jnp.transpose(xs[core, :, at])
        x_other[at, :] = jnp.transpose(xs[1 - core, :, at])
        return 0

    lax.fori_loop(0, NZ, flip, 0)
    x_over.start()
    wait_sent(1, *x_way)

    def repack(ref, j, left, right):
        parts = []
        for n in range(HELD):
            parts += [left[CAP * n : CAP * (n + 1)], right[CAP * n : CAP * (n + 1)]]
        ref[:, columns(j)] = jnp.concatenate(parts, axis=0).astype(BF16)

    def weight_rows(m, h, j):
        return w[m, h, pl.ds(2 * j, 2)].reshape(TILE, FF)

    def expert_out(j, _):
        left, right = [dot_nt(hidden[...], weight_rows(2, h, j)) for h in range(2)]
        repack(send_x, j, left, right)
        return 0

    def piece(m, way, distance):
        if m == 2:
            if distance == NZ:
                place_at = NZ - 1
            elif distance < NZ // 2 or (distance == NZ // 2 and way == 0):
                place_at = 2 * (distance - 1) + way
            elif distance == NZ // 2:
                place_at = NZ - 2
            else:
                place_at = 2 * (NZ - 1 - distance) + 1 - way
            cols = pl.ds(CHUNK * place_at, CHUNK)
            return grads_t[HIDDEN_PIECE * way : HIDDEN_PIECE * (way + 1), cols]
        chunk = lax.rem(z + (NZ - distance if way == 0 else distance), NZ)
        return grads[m, pl.ds(pl.multiple_of(chunk * CHUNK + way * PIECE, PIECE), PIECE), :]

    def slots(m, way, step):
        if m == 2:
            return ring_send_t, ring_recv_t, step * 2 + way
        return ring_send, ring_recv, (step * 2 + m) * 2 + way

    def ring(m, way, step):
        src, dst, n = slots(m, way, step)
        k = (step * 3 + m) * 2 + way
        return pltpu.make_async_remote_copy(
            src_ref=src.at[n],
            dst_ref=dst.at[n],
            send_sem=ring_ss.at[k],
            recv_sem=ring_rs.at[k],
            device_id=(after, before)[way],
        )

    def begin(m):
        for way in range(2):
            src, _, n = slots(m, way, 0)
            src[n] = piece(m, way, 1).astype(BF16)
            ring(m, way, 0).start()

    def pass_on(m, step):
        for way in range(2):
            ring(m, way, step).wait_recv()
            src, dst, n = slots(m, way, step)
            total = dst[n].astype(F32) + piece(m, way, step + 2)
            src[n + (2 if m == 2 else 4)] = total.astype(BF16)
            ring(m, way, step + 1).start()

    def finish(m):
        for way in range(2):
            ring(m, way, NZ - 2).wait_recv()
            _, dst, n = slots(m, way, NZ - 2)
            total = dst[n].astype(F32) + piece(m, way, NZ)
            if m == 2:
                cols = pl.ds(HIDDEN_PIECE * way, HIDDEN_PIECE)
                grad_w[m, :, cols] = jnp.transpose(total).astype(BF16)
            else:
                grad_w[m, PIECE * way : PIECE * (way + 1), :] = total.astype(BF16)

    def down_grad(part):
        for i in range(HELD // 2):
            dy_over(part, i).wait()
        for j in range(TILES // 2 * part, TILES // 2 * (part + 1)):
            grads_t[:, columns(j)] = dot(hidden_t[...], dys[core, :, columns(j)])

    def half_hidden_grad(part, j):
        cols = pl.ds(PART * part, PART)
        near = pl.ds(NZ // 2 * part, NZ // 2)
        terms = [
            dot(dys[h, own, cols], w[2, h, near, :, columns(j)].reshape(PART, TILE)) for h in range(2)
        ]
        return terms[0] + terms[1]

    def token_part(j):
        gate_g, up_g = rights[0, own, :], rights[1, own, :]
        left, right = [
            dot_nt(gate_g, weight_rows(0, h, j)) + dot_nt(up_g, weight_rows(1, h, j))
            for h in range(2)
        ]
        repack(send_part, j, left, right)

    def weight_grad(m):
        for j in range(FF // TILE):
            grad_over(m, j).wait()

        def one(j, _):
            grads[m, :, columns(j)] = dot(x_mine[...], rights[m, :, columns(j)])
            return 0

        lax.fori_loop(0, FF // TILE, one, 0)

    unpack(*dy_ways[0][1::2], dys, pl.ds(0, PART), lambda i: dy_over(0, i))
    hidden_over.wait()
    down_grad(0)
    begin(2)

    def first_half(j, _):
        partial[:, columns(j)] = half_hidden_grad(0, j)
        return 0

    lax.fori_loop(0, FF // TILE, first_half, 0)
    lax.fori_loop(0, TILES, expert_out, 0)
    pass_on(2, 0)
    unpack(*dy_ways[1][1::2], dys, pl.ds(PART, PART), lambda i: dy_over(1, i))
    send_blocks(everyone, -1, *out_way)
    for j in range(FF // TILE):
        hg = partial[:, columns(j)] + half_hidden_grad(1, j)
        rights[0, own, columns(j)] = (hg * acts[:, columns(j)]).astype(BF16)
        rights[1, own, columns(j)] = (hg * silus[:, columns(j)]).astype(BF16)
        grad_over(0, j).start()
        grad_over(1, j).start()
    down_grad(1)
    pass_on(2, 1)
    x_over.wait()
    weight_grad(0)
    begin(0)
    pass_on(2, 2)
    weight_grad(1)
    begin(1)
    token_part(0)
    token_part(1)
    pass_on(0, 0)
    token_part(2)
    token_part(3)
    pass_on(2, 3)
    pass_on(1, 0)
    send_blocks(everyone, -1, *part_way)
    for step in range(1, 3):
        pass_on(0, step)
        pass_on(2, step + 3)
        pass_on(1, step)

    def last_steps(step, _):
        pass_on(0, step)
        pass_on(1, step)
        return 0

    lax.fori_loop(3, NZ - 2, last_steps, 0)
    finish(2)

    for n in everyone:
        wait_block(n, recv_out, out_rs)
        wait_block(n, recv_part, part_rs)
    gate_acc[...] = jnp.zeros_like(gate_acc)

    def spread(ref, j, at, value):
        for h in range(2):
            for c in range(2):
                ref[:, at(j, c, h)] = value[
                    TOK * h : TOK * (h + 1), CHUNK * c : CHUNK * (c + 1)
                ].astype(BF16)

    def combine(j, _):
        back = recv_out[:, columns(j)]
        spread(mixed, j, near_columns, dot(prob_hi[...], back) + dot(prob_lo[...], back))
        spread(grad_tok, j, chunk_columns, dot(onehot_t[...], recv_part[:, columns(j)]))
        product = back.astype(F32) * dot(onehot_b[...], stacked(cot, j, near_columns))
        gate_acc[...] += product[:, 0:TOK] + product[:, TOK : 2 * TOK]
        return 0

    lax.fori_loop(0, TILES, combine, 0)
    inner = jnp.sum(gate_acc[...], axis=1, keepdims=True) * onehot[...]
    result = jnp.zeros((TOPK, TOK), F32)
    for n in everyone:
        both = jnp.sum(inner[BLK * n : BLK * (n + 1)], axis=0, keepdims=True)
        value = both[:, 0:TOK] + both[:, TOK : 2 * TOK]
        result = jnp.where(ids[...] == peer(n), value, result)
    grad_gate[...] = result

    finish(0)
    finish(1)
    for way in dy_ways:
        wait_sent(1, *way)
    wait_sent(-1, *out_way)
    wait_sent(-1, *part_way)

    def wait_ring(step, _):
        for m in range(3):
            for way in range(2):
                ring(m, way, step).wait_send()
        return 0

    lax.fori_loop(0, NZ - 1, wait_ring, 0)


def hand_out(*refs):
    ins, outs, sem = refs[:4], refs[4:8], refs[8]
    copies = [pltpu.make_async_copy(a, b, sem.at[n]) for n, (a, b) in enumerate(zip(ins, outs))]
    for c in copies:
        c.start()
    for c in copies:
        c.wait()


def per_device(tokens, expert_ids, gate_probs, cotangent, expert_weights):
    weights = jnp.transpose(expert_weights[:, 0], (1, 0, 2)).reshape(3, NZ, 2, CHUNK, FF)
    anywhere = pl.BlockSpec(memory_space=pl.ANY)
    dma = pltpu.SemaphoreType.DMA
    vmem = pltpu.VMEM
    results = (
        jax.ShapeDtypeStruct((TOK, D), BF16),
        jax.ShapeDtypeStruct((TOK, D), BF16),
        jax.ShapeDtypeStruct((TOPK, TOK), F32),
        jax.ShapeDtypeStruct((3, CHUNK, FF), BF16),
    )
    made = pl.pallas_call(
        moe_kernel,
        out_shape=tuple(vmem(r.shape, r.dtype) for r in results),
        in_specs=[anywhere] * 5,
        out_specs=(pl.BlockSpec(memory_space=pltpu.VMEM),) * 4,
        scratch_shapes=[
            vmem((TOK, D), BF16),
            vmem((TOPK, TOK), jnp.int32),
            vmem((TOPK, TOK), F32),
            vmem((TOK, D), BF16),
        ]
        + [
            vmem((3, 2, NZ, CHUNK, FF), BF16),
            vmem((HELD, TOK), F32),
            vmem((HELD, TOK), F32),
            vmem((PACK, 2 * TOK), F32),
            vmem((PACK, 2 * TOK), BF16),
            vmem((PACK, 2 * TOK), F32),
        ]
        + [vmem((2 * TOK, PACK), BF16)] * 3
        + [vmem((PACK, TOK), F32)]
        + [vmem((PACK, HALF), BF16), vmem((2, PACK, PART), BF16), vmem((PACK, HALF), BF16)]
        + [vmem((PACK, HALF), BF16), vmem((2, PACK, PART), BF16)]
        + [vmem((PACK, HALF), BF16)] * 2
        + [
            vmem((2, ROWS, HALF), BF16),
            vmem((2, 2 * ROWS, HALF), BF16),
            vmem((HALF, 2 * ROWS), BF16),
            vmem((HALF, ROWS), BF16),
            vmem((ROWS, FF), BF16),
            vmem((FF, 2 * ROWS), BF16),
            vmem((ROWS, FF), F32),
            vmem((ROWS, FF), F32),
            vmem((ROWS, FF), F32),
            vmem((2, 2 * ROWS, FF), BF16),
            vmem((2, HALF, FF), F32),
            vmem((FF, HALF), F32),
        ]
        + [vmem(((NZ - 1) * 4, PIECE, FF), BF16)] * 2
        + [vmem(((NZ - 1) * 2, HIDDEN_PIECE, CHUNK), BF16)] * 2
        + [dma((4,)), dma((4 + 2 * NZ,))]
        + [dma((HELD,))] * 10
        + [dma((2 + HELD + 6,))] * 2
        + [dma(((NZ - 1) * 6,))] * 2,
        compiler_params=pltpu.CompilerParams(
            collective_id=0, has_side_effects=True, vmem_limit_bytes=60 << 20
        ),
    )(tokens, expert_ids.T, gate_probs.T, cotangent, weights)
    made = [pltpu.with_memory_space_constraint(m, pltpu.VMEM) for m in made]
    mixed, grad_tok, grad_gate, grad_w = pl.pallas_call(
        hand_out,
        out_shape=results,
        in_specs=[pl.BlockSpec(memory_space=pltpu.VMEM)] * 4,
        out_specs=(anywhere,) * 4,
        scratch_shapes=[dma((4,))],
    )(*made)
    return mixed, grad_tok, grad_gate.T, jnp.transpose(grad_w, (1, 0, 2))[:, None]


def solution(mesh):
    rows = P(("dp", "expert"), None)
    return jax.shard_map(
        per_device,
        mesh=mesh,
        in_specs=(rows, rows, rows, rows, P(None, "expert", None, None)),
        out_specs=(rows, rows, rows, P("dp", "expert", None, None)),
        check_vma=False,
    )
```

```python
import jax
import jax.numpy as jnp
from jax import lax
from jax.experimental import pallas as pl
from jax.experimental.pallas import tpu as pltpu
from jax.sharding import PartitionSpec as P

CAP = 24
TOK = 128
D = 2048
HALF = 1024
FF = 768
TOPK = 8
NX, NY, NZ = 4, 4, 8
HELD = NX * NY
BLK = 2 * CAP
PACK = HELD * BLK
ROWS = HELD * CAP
TILE = 256
TILES = HALF // TILE
CHUNK = D // (2 * NZ)
SUBS = 2
PIECE = CHUNK // 2 // SUBS
HIDDEN_PIECE = FF // 2 // SUBS
PART = HALF // 2
OFFSETS = (
    (0, 0), (2, 2), (0, 2), (2, 0), (1, 2), (2, 1), (3, 2), (2, 3),
    (1, 1), (3, 3), (1, 3), (3, 1), (0, 1), (1, 0), (0, 3), (3, 0),
)
BF16 = jnp.bfloat16
F32 = jnp.float32
NT = (((1,), (1,)), ((), ()))


def dot(a, b):
    return jnp.dot(a, b, preferred_element_type=F32)


def dot_nt(a, b):
    return lax.dot_general(a, b, NT, preferred_element_type=F32)


def moe_kernel(
    tok_hbm, ids_hbm, probs_hbm, cot_hbm, w_hbm,
    mixed, grad_tok, grad_gate, grad_w,
    tok, ids, probs, cot,
    w, place, held_prob, onehot, onehot_b, prob, onehot_t, prob_hi, prob_lo, gate_acc,
    send_x, send_dy, send_part, recv_x, recv_dy, recv_out, recv_part,
    xs, dys, x_mine, x_other, hidden, hidden_t, acts, silus, partial, rights, grads, grads_t,
    ring_send, ring_recv, ring_send_t, ring_recv_t, hidden_flip,
    in_sem, w_sem, x_ss, x_rs, dy_ss, dy_rs, late_ss, late_rs, out_ss, out_rs, part_ss, part_rs,
    sib_ss, sib_rs, ring_ss, ring_rs,
):
    dp, ex = lax.axis_index("dp"), lax.axis_index("expert")
    z, core = lax.div(dp, 2), lax.rem(dp, 2)
    xx, yy = lax.div(ex, NY), lax.rem(ex, NY)

    def peer(n, way=1):
        dx, dy = OFFSETS[n]
        if way < 0:
            dx, dy = (NX - dx) % NX, (NY - dy) % NY
        return lax.rem(xx + dx, NX) * NY + lax.rem(yy + dy, NY)

    sibling = {"dp": z * 2 + (1 - core), "expert": ex}
    after = {"dp": lax.rem(z + 1, NZ) * 2 + core, "expert": ex}
    before = {"dp": lax.rem(z + NZ - 1, NZ) * 2 + core, "expert": ex}

    loads = [
        pltpu.make_async_copy(src, dst, in_sem.at[n])
        for n, (src, dst) in enumerate(
            ((ids_hbm, ids), (probs_hbm, probs), (tok_hbm, tok), (cot_hbm, cot))
        )
    ]
    for c in loads:
        c.start()
    def near_chunk(j, c):
        if c == 0:
            return lax.rem(z + NZ - 1 - j, NZ)
        return lax.rem(z + 1 + j + NZ // 2 * (j // (TILES - 1)), NZ)

    w_copies = [
        pltpu.make_async_copy(w_hbm.at[m, :, h], w.at[m, h], w_sem.at[2 * m + h])
        for m in range(2)
        for h in range(2)
    ]
    w_copies += [
        pltpu.make_async_copy(
            w_hbm.at[2, near_chunk(j, c), h], w.at[2, h, 2 * j + c], w_sem.at[4 + (2 * j + c) * 2 + h]
        )
        for j in range(TILES)
        for c in range(2)
        for h in range(2)
    ]

    barrier = pltpu.get_barrier_semaphore()
    for n in range(1, HELD):
        pl.semaphore_signal(barrier, inc=1, device_id={"dp": dp, "expert": peer(n)})
    for other in (sibling, after, before):
        pl.semaphore_signal(barrier, inc=1, device_id=other)

    loads[0].wait()
    loads[1].wait()

    held_id = lax.broadcasted_iota(jnp.int32, (HELD, TOK), 0)
    has = jnp.zeros((HELD, TOK), F32)
    chances = jnp.zeros((HELD, TOK), F32)
    for k in range(TOPK):
        hit = ids[k : k + 1, :] == held_id
        has = jnp.where(hit, 1.0, has)
        chances = chances + jnp.where(hit, probs[k : k + 1, :], 0.0)
    held_prob[...] = chances
    earlier = lax.broadcasted_iota(jnp.int32, (TOK, TOK), 0) < lax.broadcasted_iota(
        jnp.int32, (TOK, TOK), 1
    )
    count = dot(has.astype(BF16), jnp.where(earlier, 1.0, 0.0).astype(BF16))
    place[...] = jnp.where(has > 0.0, count, -1.0)
    slot = lax.broadcasted_iota(jnp.int32, (CAP, TOK), 0).astype(F32)
    zero = jnp.zeros((CAP, TOK), F32)

    def fill(ref, n, value):
        low, mid, top = BLK * n, BLK * n + CAP, BLK * (n + 1)
        ref[low:mid, 0:TOK] = value
        ref[low:mid, TOK : 2 * TOK] = zero
        ref[mid:top, 0:TOK] = zero
        ref[mid:top, TOK : 2 * TOK] = value

    def hits(n):
        return place[pl.ds(peer(n), 1), :] == slot

    def chunk_columns(j, c, h):
        return pl.ds(pl.multiple_of((4 * j + 2 * c + h) * CHUNK, CHUNK), CHUNK)

    def near_columns(j, c, h):
        return pl.ds(pl.multiple_of((2 * near_chunk(j, c) + h) * CHUNK, CHUNK), CHUNK)

    def stacked(ref, j, at):
        halves = [
            jnp.concatenate([ref[:, at(j, c, h)] for c in range(2)], axis=1) for h in range(2)
        ]
        return jnp.concatenate(halves, axis=0)

    def columns(j):
        return pl.ds(pl.multiple_of(j * TILE, TILE), TILE)

    def exchange(n, way, src, dst, send_sem, recv_sem):
        rows = pl.ds(BLK * n, BLK)
        return pltpu.make_async_remote_copy(
            src_ref=src.at[rows],
            dst_ref=dst.at[rows],
            send_sem=send_sem.at[n],
            recv_sem=recv_sem.at[n],
            device_id={"dp": dp, "expert": peer(n, way)},
        )

    def send_blocks(blocks, way, src, dst, send_sem, recv_sem):
        for n in blocks:
            if n:
                exchange(n, way, src, dst, send_sem, recv_sem).start()
            else:
                mine = pl.ds(0, BLK)
                pltpu.make_async_copy(src.at[mine], dst.at[mine], recv_sem.at[0]).start()

    def wait_sent(way, src, dst, send_sem, recv_sem):
        for n in range(1, HELD):
            exchange(n, way, src, dst, send_sem, recv_sem).wait_send()

    def wait_block(n, dst, recv_sem):
        rows = pl.ds(pl.multiple_of(n * BLK, BLK), BLK)
        pltpu.make_async_copy(dst.at[rows], dst.at[rows], recv_sem.at[n]).wait()

    x_way = (send_x, recv_x, x_ss, x_rs)
    dy_ways = (
        (send_dy.at[0], recv_dy.at[0], dy_ss, dy_rs),
        (send_dy.at[1], recv_dy.at[1], late_ss, late_rs),
    )
    out_way = (send_x, recv_out, out_ss, out_rs)
    part_way = (send_part, recv_part, part_ss, part_rs)
    everyone = range(HELD)

    for group in range(2):
        blocks = range(HELD // 2 * group, HELD // 2 * (group + 1))
        for n in blocks:
            fill(onehot, n, jnp.where(hits(n), 1.0, 0.0))
        rows = pl.ds(PACK // 2 * group, PACK // 2)
        onehot_b[rows, :] = onehot[rows, :].astype(BF16)
        if group == 0:
            loads[2].wait()
            for c in w_copies:
                c.start()

        def pack_x(j, _, rows=rows):
            send_x[rows, columns(j)] = dot(onehot_b[rows, :], stacked(tok, j, chunk_columns)).astype(BF16)
            return 0

        lax.fori_loop(0, TILES, pack_x, 0)
        if group == 0:
            pl.semaphore_wait(barrier, HELD - 1 + 3)
        send_blocks(blocks, 1, *x_way)

    for n in everyone:
        fill(prob, n, jnp.where(hits(n), held_prob[pl.ds(peer(n), 1), :], 0.0))
    row_prob = jnp.sum(prob[...], axis=1, keepdims=True)
    loads[3].wait()

    for part in range(2):
        for j in range(TILES // 2):
            picked = dot(onehot_b[...], stacked(cot, part * TILES // 2 + j, near_columns))
            send_dy[part, :, columns(j)] = (row_prob * picked).astype(BF16)
        send_blocks(everyone, 1, *dy_ways[part])

    onehot_t[...] = jnp.transpose(onehot[...]).astype(BF16)
    prob_t = jnp.transpose(prob[...])
    high = prob_t.astype(BF16)
    prob_hi[...] = high
    prob_lo[...] = (prob_t - high.astype(F32)).astype(BF16)

    own, theirs = pl.ds(0, ROWS), pl.ds(ROWS, ROWS)

    def to_sibling(n, src, dst):
        return pltpu.make_async_remote_copy(
            src_ref=src, dst_ref=dst, send_sem=sib_ss.at[n], recv_sem=sib_rs.at[n], device_id=sibling
        )

    x_over = to_sibling(0, x_other, x_mine.at[:, theirs])
    hidden_over = to_sibling(1, hidden_t.at[:, own], hidden_t.at[:, theirs])

    def dy_over(part, i):
        rows = pl.ds(pl.multiple_of(i * BLK, BLK), BLK)
        there = pl.ds(pl.multiple_of(ROWS + i * BLK, BLK), BLK)
        cols = pl.ds(PART * part, PART)
        src, dst = dys.at[1 - core, rows, cols], dys.at[1 - core, there, cols]
        return to_sibling(2 + HELD // 2 * part + i, src, dst)

    def grad_over(m, j):
        src, dst = rights.at[m, own, columns(j)], rights.at[m, theirs, columns(j)]
        return to_sibling(2 + HELD + 3 * m + j, src, dst)

    def unpack(recv, recv_sem, full, cols, then=None):
        def one(i, _):
            wait_block(2 * i, recv, recv_sem)
            wait_block(2 * i + 1, recv, recv_sem)
            v = recv[pl.ds(pl.multiple_of(i * 2 * BLK, 2 * BLK), 2 * BLK), :].astype(F32)
            rows = pl.ds(pl.multiple_of(i * BLK, BLK), BLK)
            for h in range(2):
                parts = [v[CAP * (2 * b + h) : CAP * (2 * b + h + 1)] for b in range(2)]
                full[h, rows, cols] = jnp.concatenate(parts, axis=0).astype(BF16)
            if then is not None:
                then(i).start()
            return 0

        lax.fori_loop(0, HELD // 2, one, 0)

    def weight(m, h, j):
        return w[m, h, :, :, columns(j)].reshape(HALF, TILE)

    unpack(recv_x, x_rs, xs, pl.ds(0, HALF))
    for c in w_copies:
        c.wait()

    def project(j, _):
        g = dot(xs[0], weight(0, 0, j)) + dot(xs[1], weight(0, 1, j))
        u = dot(xs[0], weight(1, 0, j)) + dot(xs[1], weight(1, 1, j))
        s = jax.nn.sigmoid(g)
        silu = g * s
        units = (silu * u).astype(BF16)
        hidden[:, columns(j)] = units
        hidden_t[columns(j), own] = jnp.transpose(units)
        acts[:, columns(j)] = u * s * (1.0 + g * (1.0 - s))
        silus[:, columns(j)] = silu
        return 0

    lax.fori_loop(0, FF // TILE, project, 0)
    hidden_over.start()

    def flip(c, _):
        at = pl.ds(pl.multiple_of(c * CHUNK, CHUNK), CHUNK)
        x_mine[at, own] = jnp.transpose(xs[core, :, at])
        x_other[at, :] = jnp.transpose(xs[1 - core, :, at])
        return 0

    lax.fori_loop(0, NZ, flip, 0)
    x_over.start()
    wait_sent(1, *x_way)

    def repack(ref, j, left, right):
        parts = []
        for n in range(HELD):
            parts += [left[CAP * n : CAP * (n + 1)], right[CAP * n : CAP * (n + 1)]]
        ref[:, columns(j)] = jnp.concatenate(parts, axis=0).astype(BF16)

    def weight_rows(m, h, j):
        return w[m, h, pl.ds(2 * j, 2)].reshape(TILE, FF)

    def expert_out(j, _):
        left, right = [dot_nt(hidden[...], weight_rows(2, h, j)) for h in range(2)]
        repack(send_x, j, left, right)
        return 0

    def piece(m, way, sub, distance):
        if m == 2:
            if distance == NZ:
                place_at = NZ - 1
            elif distance < NZ // 2 or (distance == NZ // 2 and way == 0):
                place_at = 2 * (distance - 1) + way
            elif distance == NZ // 2:
                place_at = NZ - 2
            else:
                place_at = 2 * (NZ - 1 - distance) + 1 - way
            cols = pl.ds(CHUNK * place_at, CHUNK)
            return grads_t[pl.ds(HIDDEN_PIECE * (SUBS * way + sub), HIDDEN_PIECE), cols]
        chunk = lax.rem(z + (NZ - distance if way == 0 else distance), NZ)
        first = chunk * CHUNK + (SUBS * way + sub) * PIECE
        return grads[m, pl.ds(pl.multiple_of(first, PIECE), PIECE), :]

    def slots(m, way, sub, step):
        if m == 2:
            return ring_send_t, ring_recv_t, (step * 2 + way) * SUBS + sub
        return ring_send, ring_recv, ((step * 2 + m) * 2 + way) * SUBS + sub

    def ring(m, way, sub, step):
        src, dst, n = slots(m, way, sub, step)
        k = ((step * 3 + m) * 2 + way) * SUBS + sub
        return pltpu.make_async_remote_copy(
            src_ref=src.at[n],
            dst_ref=dst.at[n],
            send_sem=ring_ss.at[k],
            recv_sem=ring_rs.at[k],
            device_id=(after, before)[way],
        )

    both_ways = [(way, sub) for sub in range(SUBS) for way in range(2)]

    def begin(m):
        for way, sub in both_ways:
            src, _, n = slots(m, way, sub, 0)
            src[n] = piece(m, way, sub, 1).astype(BF16)
            ring(m, way, sub, 0).start()

    def pass_on(m, step):
        for way, sub in both_ways:
            ring(m, way, sub, step).wait_recv()
            src, dst, n = slots(m, way, sub, step)
            total = dst[n].astype(F32) + piece(m, way, sub, step + 2)
            src[n + (2 if m == 2 else 4) * SUBS] = total.astype(BF16)
            ring(m, way, sub, step + 1).start()

    def finish(m):
        for way, sub in both_ways:
            ring(m, way, sub, NZ - 2).wait_recv()
            _, dst, n = slots(m, way, sub, NZ - 2)
            total = dst[n].astype(F32) + piece(m, way, sub, NZ)
            k = SUBS * way + sub
            if m == 2:
                hidden_flip[pl.ds(HIDDEN_PIECE * k, HIDDEN_PIECE), :] = total
            else:
                grad_w[m, pl.ds(PIECE * k, PIECE), :] = total.astype(BF16)
        if m == 2:
            grad_w[m] = jnp.transpose(hidden_flip[...]).astype(BF16)

    def down_grad(part):
        for i in range(HELD // 2):
            dy_over(part, i).wait()
        for j in range(TILES // 2 * part, TILES // 2 * (part + 1)):
            grads_t[:, columns(j)] = dot(hidden_t[...], dys[core, :, columns(j)])

    def half_hidden_grad(part, j):
        cols = pl.ds(PART * part, PART)
        near = pl.ds(NZ // 2 * part, NZ // 2)
        terms = [
            dot(dys[h, own, cols], w[2, h, near, :, columns(j)].reshape(PART, TILE)) for h in range(2)
        ]
        return terms[0] + terms[1]

    def token_part(j):
        gate_g, up_g = rights[0, own, :], rights[1, own, :]
        left, right = [
            dot_nt(gate_g, weight_rows(0, h, j)) + dot_nt(up_g, weight_rows(1, h, j))
            for h in range(2)
        ]
        repack(send_part, j, left, right)

    def weight_grad(m):
        for j in range(FF // TILE):
            grad_over(m, j).wait()

        def one(j, _):
            grads[m, :, columns(j)] = dot(x_mine[...], rights[m, :, columns(j)])
            return 0

        lax.fori_loop(0, FF // TILE, one, 0)

    unpack(*dy_ways[0][1::2], dys, pl.ds(0, PART), lambda i: dy_over(0, i))
    hidden_over.wait()
    down_grad(0)
    begin(2)

    def first_half(j, _):
        partial[:, columns(j)] = half_hidden_grad(0, j)
        return 0

    lax.fori_loop(0, FF // TILE, first_half, 0)
    lax.fori_loop(0, TILES, expert_out, 0)
    pass_on(2, 0)
    unpack(*dy_ways[1][1::2], dys, pl.ds(PART, PART), lambda i: dy_over(1, i))
    send_blocks(everyone, -1, *out_way)
    for j in range(FF // TILE):
        hg = partial[:, columns(j)] + half_hidden_grad(1, j)
        rights[0, own, columns(j)] = (hg * acts[:, columns(j)]).astype(BF16)
        rights[1, own, columns(j)] = (hg * silus[:, columns(j)]).astype(BF16)
        grad_over(0, j).start()
        grad_over(1, j).start()
    down_grad(1)
    pass_on(2, 1)
    x_over.wait()
    weight_grad(0)
    begin(0)
    pass_on(2, 2)
    weight_grad(1)
    begin(1)
    token_part(0)
    pass_on(0, 0)
    token_part(1)
    pass_on(2, 3)
    token_part(2)
    pass_on(1, 0)
    token_part(3)
    send_blocks(everyone, -1, *part_way)
    for step in range(1, 3):
        pass_on(0, step)
        pass_on(2, step + 3)
        pass_on(1, step)

    def last_steps(step, _):
        pass_on(0, step)
        pass_on(1, step)
        return 0

    lax.fori_loop(3, NZ - 2, last_steps, 0)
    finish(2)

    for n in everyone:
        wait_block(n, recv_out, out_rs)
        wait_block(n, recv_part, part_rs)
    gate_acc[...] = jnp.zeros_like(gate_acc)

    def spread(ref, j, at, value):
        for h in range(2):
            for c in range(2):
                ref[:, at(j, c, h)] = value[
                    TOK * h : TOK * (h + 1), CHUNK * c : CHUNK * (c + 1)
                ].astype(BF16)

    def combine(j, _):
        back = recv_out[:, columns(j)]
        spread(mixed, j, near_columns, dot(prob_hi[...], back) + dot(prob_lo[...], back))
        spread(grad_tok, j, chunk_columns, dot(onehot_t[...], recv_part[:, columns(j)]))
        product = back.astype(F32) * dot(onehot_b[...], stacked(cot, j, near_columns))
        gate_acc[...] += product[:, 0:TOK] + product[:, TOK : 2 * TOK]
        return 0

    lax.fori_loop(0, TILES, combine, 0)
    inner = jnp.sum(gate_acc[...], axis=1, keepdims=True) * onehot[...]
    result = jnp.zeros((TOPK, TOK), F32)
    for n in everyone:
        both = jnp.sum(inner[BLK * n : BLK * (n + 1)], axis=0, keepdims=True)
        value = both[:, 0:TOK] + both[:, TOK : 2 * TOK]
        result = jnp.where(ids[...] == peer(n), value, result)
    grad_gate[...] = result

    finish(0)
    finish(1)
    for way in dy_ways:
        wait_sent(1, *way)
    wait_sent(-1, *out_way)
    wait_sent(-1, *part_way)

    def wait_ring(step, _):
        for m in range(3):
            for way, sub in both_ways:
                ring(m, way, sub, step).wait_send()
        return 0

    lax.fori_loop(0, NZ - 1, wait_ring, 0)


def hand_out(*refs):
    ins, outs, sem = refs[:4], refs[4:8], refs[8]
    copies = [pltpu.make_async_copy(a, b, sem.at[n]) for n, (a, b) in enumerate(zip(ins, outs))]
    for c in copies:
        c.start()
    for c in copies:
        c.wait()


def per_device(tokens, expert_ids, gate_probs, cotangent, expert_weights):
    weights = jnp.transpose(expert_weights[:, 0], (1, 0, 2)).reshape(3, NZ, 2, CHUNK, FF)
    anywhere = pl.BlockSpec(memory_space=pl.ANY)
    dma = pltpu.SemaphoreType.DMA
    vmem = pltpu.VMEM
    results = (
        jax.ShapeDtypeStruct((TOK, D), BF16),
        jax.ShapeDtypeStruct((TOK, D), BF16),
        jax.ShapeDtypeStruct((TOPK, TOK), F32),
        jax.ShapeDtypeStruct((3, CHUNK, FF), BF16),
    )
    made = pl.pallas_call(
        moe_kernel,
        out_shape=tuple(vmem(r.shape, r.dtype) for r in results),
        in_specs=[anywhere] * 5,
        out_specs=(pl.BlockSpec(memory_space=pltpu.VMEM),) * 4,
        scratch_shapes=[
            vmem((TOK, D), BF16),
            vmem((TOPK, TOK), jnp.int32),
            vmem((TOPK, TOK), F32),
            vmem((TOK, D), BF16),
        ]
        + [
            vmem((3, 2, NZ, CHUNK, FF), BF16),
            vmem((HELD, TOK), F32),
            vmem((HELD, TOK), F32),
            vmem((PACK, 2 * TOK), F32),
            vmem((PACK, 2 * TOK), BF16),
            vmem((PACK, 2 * TOK), F32),
        ]
        + [vmem((2 * TOK, PACK), BF16)] * 3
        + [vmem((PACK, TOK), F32)]
        + [vmem((PACK, HALF), BF16), vmem((2, PACK, PART), BF16), vmem((PACK, HALF), BF16)]
        + [vmem((PACK, HALF), BF16), vmem((2, PACK, PART), BF16)]
        + [vmem((PACK, HALF), BF16)] * 2
        + [
            vmem((2, ROWS, HALF), BF16),
            vmem((2, 2 * ROWS, HALF), BF16),
            vmem((HALF, 2 * ROWS), BF16),
            vmem((HALF, ROWS), BF16),
            vmem((ROWS, FF), BF16),
            vmem((FF, 2 * ROWS), BF16),
            vmem((ROWS, FF), F32),
            vmem((ROWS, FF), F32),
            vmem((ROWS, FF), F32),
            vmem((2, 2 * ROWS, FF), BF16),
            vmem((2, HALF, FF), F32),
            vmem((FF, HALF), F32),
        ]
        + [vmem(((NZ - 1) * 4 * SUBS, PIECE, FF), BF16)] * 2
        + [vmem(((NZ - 1) * 2 * SUBS, HIDDEN_PIECE, CHUNK), BF16)] * 2
        + [vmem((FF, CHUNK), F32)]
        + [dma((4,)), dma((4 + 2 * NZ,))]
        + [dma((HELD,))] * 10
        + [dma((2 + HELD + 6,))] * 2
        + [dma(((NZ - 1) * 6 * SUBS,))] * 2,
        compiler_params=pltpu.CompilerParams(
            collective_id=0, has_side_effects=True, vmem_limit_bytes=60 << 20
        ),
    )(tokens, expert_ids.T, gate_probs.T, cotangent, weights)
    made = [pltpu.with_memory_space_constraint(m, pltpu.VMEM) for m in made]
    mixed, grad_tok, grad_gate, grad_w = pl.pallas_call(
        hand_out,
        out_shape=results,
        in_specs=[pl.BlockSpec(memory_space=pltpu.VMEM)] * 4,
        out_specs=(anywhere,) * 4,
        scratch_shapes=[dma((4,))],
    )(*made)
    return mixed, grad_tok, grad_gate.T, jnp.transpose(grad_w, (1, 0, 2))[:, None]


def solution(mesh):
    rows = P(("dp", "expert"), None)
    return jax.shard_map(
        per_device,
        mesh=mesh,
        in_specs=(rows, rows, rows, rows, P(None, "expert", None, None)),
        out_specs=(rows, rows, rows, P("dp", "expert", None, None)),
        check_vma=False,
    )
```
